32 devices in a mesh: dp: 2 (over x), seq: 8 (over z, y), head: 2 (over core).
Axes of the slice: x: 2, y: 2, z: 4, core: 2. Of those that a mesh axis runs over, the one named last changes fastest.
Arguments:
- queries: bfloat16 [3072, 2048], P(('dp', 'seq'), 'head'), parts along dimension 0, may hold values from -6 to 6
- keys: bfloat16 [3072, 2048], P(('dp', 'seq'), 'head'), parts along dimension 0, may hold values from -6 to 6
- values: bfloat16 [3072, 2048], P(('dp', 'seq'), 'head'), parts along dimension 0, may hold values from -6 to 6
- segments: int32 [3072], P(('dp', 'seq')), parts along dimension 0, may hold values from 0 to 2, never falling along the last dimension, each value on 1 to 768 neighbouring positions
- hidden_in: bfloat16 [3072, 2048], P(('dp', 'seq', 'head')), parts along dimension 0, may hold values from -6 to 6
- attn_gain: float32 [2048], P('head'), may hold values from 0.25 to 1.75
- out_proj: bfloat16 [2048, 2048], P('head', 'seq'), may hold values from -0.125 to 0.125
- moe_gain: float32 [2048], replicated, may hold values from 0.1 to 1.9
- route_ids: int32 [3072, 8], P(('dp', 'seq', 'head')), parts along dimension 0, may hold values from 0 to 15, all different within a row; in each aligned block of 96 rows (0 to 95, 96 to 191, ...) at most 64 rows name the same one
- route_w: float32 [3072, 8], P(('dp', 'seq', 'head')), parts along dimension 0, may hold values from 0.02 to 0.5
- w_gate: bfloat16 [16, 2048, 768], P(('seq', 'head')), may hold values from -0.125 to 0.125
- w_up: bfloat16 [16, 2048, 768], P(('seq', 'head')), may hold values from -0.125 to 0.125
- w_down: bfloat16 [16, 768, 2048], P(('seq', 'head')), may hold values from -0.625 to 0.625
Outputs:
- block_out: bfloat16 [3072, 2048], P(('dp', 'seq', 'head')), parts along dimension 0
The draws below stay inside these ranges and needn't reach their ends.
There are 2 independent parts, one for each index of `dp`. The reference program is written for one: setup_inputs(seed, part) draws one part's arguments, and reference() takes and returns one part's arrays. A program takes and returns all parts, laid end to end along the dimension named above; an argument that names none is the same for every part. Nothing has to cross between parts.
Inputs may be any that keep to these rules, and one draw needn't show every extreme that they name: `route_ids`: each row names 8 different experts. In the 96 rows of one device no expert is named more than 64 times; in some device's rows some expert is named exactly 64 times. `segments`: ids of 3 packed documents, never falling, every document at least one token, the longest exactly 768 tokens.
All inputs are finite; a program needn't handle non-finite values.
Results may differ from the reference program's by a relative error of at most 0.0065.
Values may be sent and summed in bfloat16 or wider, within the bound.
A program may use at most 128 MiB of HBM per device.

```python
import math
import jax
import jax.numpy as jnp
import numpy as np
from jax import lax

D = 2048
DK = 128
FF = 768
TOPK = 8
HEADS = 16
DOCS = 3
TOKENS = 1536
TOK_DEV = 96
EXPERTS = 16
CAP = 64


def level_of(rng, extent, shards, least, largest):
    gain, own = 1.0, jax.random.fold_in(rng, 6)
    for dim, shards_of in shards:
        heights = jnp.exp(jax.random.uniform(jax.random.fold_in(own, dim), (shards_of,), jnp.float32, least / len(shards), largest / len(shards)))
        gain = gain * jnp.repeat(heights, extent[dim] // shards_of).reshape([-1 if axis == dim else 1 for axis in range(len(extent))])
    return gain


def length_profile(count, total, most, lean):
    loads = [(1 << 20) // math.isqrt(rank ** lean) + 1 for rank in range(2, count + 1)]
    spare, given = total - most - (count - 1), [1] * (count - 1)
    while spare > 0:
        free = [i for i in range(count - 1) if given[i] < most]
        pool, left = sum([loads[i] for i in free]), spare
        for i in free:
            extra = min(most - given[i], max(1, left * loads[i] // pool), spare)
            given[i] = given[i] + extra
            spare = spare - extra
    return np.array([most] + given)


def uneven_parts(key, number_of, total, reach, skew):
    if number_of == 2:
        one = jax.random.randint(key, (), max(1, total - reach), min(reach, total - 1) + 1)
        return jnp.stack([one, total - one])
    lengths = jnp.asarray(length_profile(number_of, total, reach, skew), jnp.int32)
    pairs = (number_of - 1) // 2
    donor, sink = lengths[1:1 + 2 * pairs:2], lengths[2:2 + 2 * pairs:2]
    slack = jnp.minimum(donor - 1, reach - sink)
    shifted = jax.random.randint(jax.random.fold_in(key, 1), (pairs,), 0, 1 << 20) % (slack + 1)
    lengths = lengths.at[1:1 + 2 * pairs:2].set(donor - shifted).at[2:2 + 2 * pairs:2].set(sink + shifted)
    return lengths[jax.random.permutation(jax.random.fold_in(key, 2), number_of)]


def shared_out(key, own, number, rows, amount, top, most, skew):
    sequence = jax.random.permutation(key, amount)
    packed, ordinary = load_shares(amount, rows * top, most, skew, True), load_shares(amount, rows * top, most, skew, False)
    places = jnp.arange(amount)

    def named(sizes, turn):
        used = int((sizes > 0).sum())
        fixed = max(1, used // 4)
        moved = fixed + (places - fixed + turn * (used - fixed)) % max(1, amount - fixed)
        return jnp.zeros((amount,), jnp.int32).at[sequence[jnp.where(places < fixed, places, moved)]].set(jnp.asarray(sizes, jnp.int32))

    sizes = jnp.where(number % 4 == 0, named(packed, number // 4), named(ordinary, number - number // 4 - 1))
    mixed = jax.random.permutation(jax.random.fold_in(own, 3), amount)
    donor, taker = mixed[0:amount // 2 * 2:2], mixed[1:amount // 2 * 2:2]
    margin = jnp.minimum(sizes[donor] - 1, most - sizes[taker]) // 2
    margin = jnp.where((donor == sequence[0]) | (taker == sequence[0]) | (sizes[taker] == 0), 0, jnp.maximum(margin, 0))
    moved = jax.random.randint(jax.random.fold_in(own, 4), (amount // 2,), 0, 1 << 20) % (margin + 1)
    sizes = sizes.at[donor].add(-moved).at[taker].add(moved)
    members = jnp.searchsorted(jnp.cumsum(sizes), jnp.arange(rows * top), side="right").astype(jnp.int32)
    table = members.reshape(top, rows).T
    table = table[jax.random.permutation(jax.random.fold_in(own, 1), rows)]
    turn = jax.random.randint(jax.random.fold_in(own, 2), (rows, 1), 0, top)
    return jnp.take_along_axis(table, (jnp.arange(top)[None, :] + turn) % top, axis=1)


def load_shares(count, total, bound, skew, full):
    weights = [(1 << 20) // math.isqrt(rank ** skew) + 1 for rank in range(1, count + 1)]
    largest = bound if full else min(bound, max(-(-total // count), total * weights[0] // sum(weights)))
    least = 1 if total - largest >= count - 1 else 0
    given, rest = [largest] + [least] * (count - 1), total - largest - least * (count - 1)
    while rest > 0:
        candidates = [i for i in range(1, count) if given[i] < largest] or [i for i in range(1, count) if given[i] < bound]
        mass, budget = sum([weights[i] for i in candidates]), rest
        for i in candidates:
            extra = min(bound - given[i], max(1, budget * weights[i] // mass), rest)
            given[i] = given[i] + extra
            rest = rest - extra
    return np.array(given)


def normal_values(key, extent, spread, most, shards=(), held_as=jnp.bfloat16):
    array = jax.random.normal(key, extent, jnp.float32) * spread
    if len(shards) > 0:
        array = level_of(key, extent, shards, -0.22, 0.18) * array
    return jnp.clip(array, min=-most, max=most).astype(held_as)


def setup_inputs(seed: int = 0, part: int = 0) -> dict:
    key_of = jax.random.split(jax.random.key(seed), 14)
    own_keys = jax.random.split(jax.random.fold_in(key_of[13], part), 14)
    queries = normal_values(own_keys[0], (TOKENS, HEADS * DK), 1.0, 6.0, ((0, 8), (1, 2)))
    keys = normal_values(own_keys[1], (TOKENS, HEADS * DK), 1.0, 6.0, ((0, 8), (1, 2)))
    values = normal_values(own_keys[2], (TOKENS, HEADS * DK), 1.0, 6.0, ((0, 8), (1, 2)))
    segments = jnp.searchsorted(jnp.cumsum(uneven_parts(own_keys[3], DOCS, TOKENS, TOKENS // 2, 0)), jnp.arange(TOKENS), side="right").astype(jnp.int32)
    hidden_in = normal_values(own_keys[4], (TOKENS, D), 1.0, 6.0, ((0, 16),))
    attn_gain = jnp.clip(1.0 + 0.15 * jax.random.normal(key_of[5], (HEADS * DK,), jnp.float32), 0.25, 1.75)
    out_proj = normal_values(key_of[6], (HEADS * DK, D), (HEADS * DK) ** -0.5, 0.125, ((0, 2), (1, 8)))
    moe_gain = jnp.clip(1.0 + 0.18 * jax.random.normal(key_of[7], (D,), jnp.float32), 0.1, 1.9)
    route_ids_keys = jax.random.split(jax.random.fold_in(own_keys[8], 1), TOKENS // TOK_DEV)
    route_ids_turns = jax.random.permutation(jax.random.fold_in(own_keys[8], 3), TOKENS // TOK_DEV)
    route_ids = jax.vmap(lambda own, number: shared_out(jax.random.fold_in(own_keys[8], 2), own, number, TOK_DEV, EXPERTS, TOPK, CAP, 3))(route_ids_keys, route_ids_turns).reshape((TOKENS, TOPK))
    route_w = jnp.clip(jnp.exp(math.log(0.5) - 3.218876 * jax.random.uniform(own_keys[9], (TOKENS, TOPK), jnp.float32) ** level_of(own_keys[9], (TOKENS, TOPK), ((0, 16),), -0.2, 0.2)), 0.02, 0.5)
    w_gate = normal_values(key_of[10], (EXPERTS, D, FF), D ** -0.5, 0.125, ((0, 16),))
    w_up = normal_values(key_of[11], (EXPERTS, D, FF), D ** -0.5, 0.125, ((0, 16),))
    w_down = normal_values(key_of[12], (EXPERTS, FF, D), (FF // 8) ** -0.5, 0.625, ((0, 16),))
    return {"queries": queries, "keys": keys, "values": values, "segments": segments, "hidden_in": hidden_in, "attn_gain": attn_gain, "out_proj": out_proj, "moe_gain": moe_gain, "route_ids": route_ids, "route_w": route_w, "w_gate": w_gate, "w_up": w_up, "w_down": w_down}


epsilon = 1e-06

def attention(queries, keys, values, segments):
    block_len = math.gcd(TOKENS, 512)
    block_count = TOKENS // block_len
    query_f = queries.astype(jnp.float32).reshape(block_count, block_len, HEADS, DK)
    key_f = keys.astype(jnp.float32).reshape(block_count, block_len, HEADS, DK)
    value_f = values.astype(jnp.float32).reshape(block_count, block_len, HEADS, DK)
    seg_blocks = segments.reshape(block_count, block_len)
    position = jnp.arange(block_len)
    causal = position[:, None] >= position[None, :]

    def block_step(carried, inputs):
        kv_state, last_seg = carried
        query_rows, key_rows, value_rows, seg_rows = inputs
        same_doc = (seg_rows[:, None] == seg_rows[None, :]) & causal
        scores = jnp.einsum('thd,shd->hts', query_rows, key_rows, precision=lax.Precision.HIGHEST)
        scores = jnp.where(same_doc[None], scores, 0.0)
        local_part = jnp.einsum('hts,shd->thd', scores, value_rows, precision=lax.Precision.HIGHEST)
        continued = (seg_rows == last_seg)[:, None, None]
        carried_part = jnp.einsum('thd,hde->the', query_rows, kv_state, precision=lax.Precision.HIGHEST)
        attn_out = local_part + jnp.where(continued, carried_part, 0.0)
        tail_mask = (seg_rows == seg_rows[-1])[:, None, None]
        tail_keys = jnp.where(tail_mask, key_rows, 0.0)
        new_state = jnp.einsum('thd,the->hde', tail_keys, value_rows, precision=lax.Precision.HIGHEST)
        new_state = new_state + jnp.where(seg_rows[-1] == last_seg, kv_state, 0.0)
        return ((new_state, seg_rows[-1]), attn_out)
    start = (jnp.zeros((HEADS, DK, DK), jnp.float32), jnp.int32(-1))
    unused, outputs = lax.scan(block_step, start, (query_f, key_f, value_f, seg_blocks))
    return outputs.reshape(TOKENS, HEADS, DK)

def reference(queries, keys, values, segments, hidden_in, attn_gain, out_proj, moe_gain, route_ids, route_w, w_gate, w_up, w_down):
    attn_raw = attention(queries, keys, values, segments)
    mean_square = lax.optimization_barrier(jnp.mean(attn_raw * attn_raw, axis=-1, keepdims=True))
    attended = attn_raw * lax.rsqrt(mean_square + epsilon) * attn_gain.reshape(HEADS, DK)
    attended = attended.astype(jnp.bfloat16).reshape(TOKENS, HEADS * DK)
    attn_out = jnp.dot(attended, out_proj, preferred_element_type=jnp.float32)
    mid = (hidden_in.astype(jnp.float32) + attn_out).astype(jnp.bfloat16)
    mid_wide = mid.astype(jnp.float32)
    mid_square = lax.optimization_barrier(jnp.mean(mid_wide * mid_wide, axis=-1, keepdims=True))
    normed = (mid_wide * lax.rsqrt(mid_square + epsilon) * moe_gain).astype(jnp.bfloat16)
    weights = route_w / lax.optimization_barrier(jnp.sum(route_w, axis=1, keepdims=True))
    max_rows = CAP * EXPERTS

    def expert_step(running, inputs):
        expert_index, gate_matrix, up_matrix, down_matrix = inputs
        route_hits = route_ids == expert_index
        weight_row = lax.optimization_barrier(jnp.sum(jnp.where(route_hits, weights, 0.0), axis=1))
        chosen = jnp.any(route_hits, axis=1)
        picked = jnp.nonzero(chosen, size=max_rows, fill_value=0)[0].astype(jnp.int32)
        live_count = jnp.sum(chosen.astype(jnp.int32))
        live_mask = jnp.arange(max_rows, dtype=jnp.int32) < live_count
        rows_in = normed[picked]
        gate_part = jnp.dot(rows_in, gate_matrix, preferred_element_type=jnp.float32)
        up_part = jnp.dot(rows_in, up_matrix, preferred_element_type=jnp.float32)
        inner = (jax.nn.silu(gate_part) * up_part).astype(jnp.bfloat16)
        expert_out = jnp.dot(inner, down_matrix, preferred_element_type=jnp.float32).astype(jnp.bfloat16)
        row_weight = jnp.where(live_mask, weight_row[picked], 0.0)
        running = running.at[picked].add(expert_out.astype(jnp.float32) * row_weight[:, None])
        return (running, None)
    indices = jnp.arange(EXPERTS, dtype=jnp.int32)
    mixture, unused = lax.scan(expert_step, jnp.zeros((TOKENS, D), jnp.float32), (indices, w_gate, w_up, w_down))
    return (mid_wide + mixture).astype(jnp.bfloat16)
```

```python
import jax
import jax.numpy as jnp
from jax import lax
from jax.sharding import PartitionSpec as P

D = 2048
DK = 128

epsilon = 1e-06


def local(
    queries,
    keys,
    values,
    segments,
    hidden_in,
    attn_gain,
    out_proj,
    moe_gain,
    route_ids,
    route_w,
    w_gate,
    w_up,
    w_down,
):
    tok_rows = queries.shape[0]
    heads_here = attn_gain.shape[0] // DK
    query_rows = queries.reshape(tok_rows, heads_here, DK)
    key_rows = keys.reshape(tok_rows, heads_here, DK)
    value_rows = values.reshape(tok_rows, heads_here, DK)
    position = jnp.arange(tok_rows)
    causal = position[:, None] >= position[None, :]
    same_doc = (segments[:, None] == segments[None, :]) & causal
    tail_mask = (segments == segments[-1])[:, None, None]
    tail_keys = jnp.where(tail_mask, key_rows, jnp.zeros_like(key_rows))
    own_state = jnp.einsum(
        "thd,the->hde", tail_keys, value_rows, preferred_element_type=jnp.float32
    ).astype(jnp.bfloat16)
    last_seg = jnp.broadcast_to(segments[-1].astype(jnp.bfloat16), (1, DK, DK))
    payload = jnp.concatenate([own_state, last_seg], axis=0)
    gathered = lax.all_gather(payload, "seq")
    before = jnp.arange(gathered.shape[0]) < lax.axis_index("seq")
    opened = gathered[:, heads_here, 0, 0] == segments[0].astype(jnp.bfloat16)
    keep = (before & opened)[:, None, None, None]
    prefix_state = jnp.sum(
        jnp.where(keep, gathered[:, :heads_here].astype(jnp.float32), 0.0), axis=0
    ).astype(jnp.bfloat16)
    scores = jnp.einsum("thd,shd->hts", query_rows, key_rows, preferred_element_type=jnp.float32)
    scores = jnp.where(same_doc[None], scores, 0.0).astype(jnp.bfloat16)
    local_part = jnp.einsum("hts,shd->thd", scores, value_rows, preferred_element_type=jnp.float32)
    continued = (segments == segments[0])[:, None, None]
    carried_part = jnp.einsum(
        "thd,hde->the", query_rows, prefix_state, preferred_element_type=jnp.float32
    )
    attn_raw = local_part + jnp.where(continued, carried_part, 0.0)
    mean_square = jnp.mean(attn_raw * attn_raw, axis=-1, keepdims=True)
    attended = attn_raw * lax.rsqrt(mean_square + epsilon) * attn_gain.reshape(heads_here, DK)
    attended = attended.astype(jnp.bfloat16).reshape(tok_rows, heads_here * DK)
    partial_out = jnp.dot(
        attended,
        lax.all_gather(out_proj, "seq", axis=1, tiled=True),
        preferred_element_type=jnp.float32,
    )
    attn_out = lax.psum_scatter(partial_out, "head", scatter_dimension=0, tiled=True)
    mid_wide = (hidden_in.astype(jnp.float32) + attn_out).astype(jnp.bfloat16).astype(jnp.float32)
    mid_square = jnp.mean(mid_wide * mid_wide, axis=-1, keepdims=True)
    normed = (mid_wide * lax.rsqrt(mid_square + epsilon) * moe_gain).astype(jnp.bfloat16)
    weights = route_w / jnp.sum(route_w, axis=1, keepdims=True)
    experts = lax.axis_size("seq") * lax.axis_size("head")
    labels = jnp.arange(experts, dtype=jnp.int32)
    dense = jnp.sum(
        jnp.where(route_ids[:, :, None] == labels[None, None, :], weights[:, :, None], 0.0), axis=1
    )
    everywhere = ("seq", "head")
    dense_all = lax.all_gather(dense, everywhere, axis=0, tiled=True)
    mine = lax.axis_index(everywhere)
    row_weight = jnp.sum(jnp.where(labels[None, :] == mine, dense_all, 0.0), axis=1, keepdims=True)
    rows_all = lax.all_gather(normed, everywhere, axis=0, tiled=True)
    gate_part = jnp.dot(rows_all, w_gate[0], preferred_element_type=jnp.float32)
    up_part = jnp.dot(rows_all, w_up[0], preferred_element_type=jnp.float32)
    inner = (jax.nn.silu(gate_part) * up_part).astype(jnp.bfloat16)
    answer = jnp.dot(inner, w_down[0], preferred_element_type=jnp.float32)
    answer = (answer * row_weight).astype(jnp.bfloat16)
    mixture = lax.psum_scatter(answer, everywhere, scatter_dimension=0, tiled=True)
    return (mid_wide + mixture.astype(jnp.float32)).astype(jnp.bfloat16)


def solution(mesh):
    return jax.shard_map(
        local,
        mesh=mesh,
        in_specs=(
            P(("dp", "seq"), "head"),
            P(("dp", "seq"), "head"),
            P(("dp", "seq"), "head"),
            P(("dp", "seq")),
            P(("dp", "seq", "head"), None),
            P("head"),
            P("head", "seq"),
            P(),
            P(("dp", "seq", "head"), None),
            P(("dp", "seq", "head"), None),
            P(("seq", "head"), None, None),
            P(("seq", "head"), None, None),
            P(("seq", "head"), None, None),
        ),
        out_specs=P(("dp", "seq", "head"), None),
        check_vma=False,
    )
```

```python
import functools

import jax
import jax.numpy as jnp
from jax import lax
from jax.experimental import pallas as pl
from jax.experimental.pallas import tpu as pltpu
from jax.sharding import PartitionSpec as P

D = 2048
DK = 128

epsilon = 1e-06


def gather_kernel(n_seq, cores, block, out, own_sem, send_sem, recv_sem):
    place, core = lax.axis_index("seq"), lax.axis_index("head")
    length = n_seq // 2
    far, near = place // 2, place % 2
    other = 1 - near

    def slot(row, col, of):
        return (row * 2 + col) * cores + (of if cores > 1 else 0)

    def send(way, src, at, row, col, of):
        return pltpu.make_async_remote_copy(
            src_ref=src,
            dst_ref=out.at[at],
            send_sem=send_sem.at[way, at],
            recv_sem=recv_sem.at[at],
            device_id={"seq": row * 2 + col, "head": of},
            device_id_type=pl.DeviceIdType.MESH,
        )

    def arrive(at):
        send(0, out.at[at], at, far, other, core).wait_recv()

    def up(src, at):
        return send(0, src, at, far + 1, near, core)

    def down(src, at):
        return send(1, src, at, far - 1, near, core)

    def across(src, at):
        return send(2, src, at, far, other, core)

    def beside(src, at):
        return send(3, src, at, far, near, 1 - core)

    barrier = pltpu.get_barrier_semaphore()

    def greet(row, col, of):
        pl.semaphore_signal(
            barrier,
            inc=1,
            device_id={"seq": row * 2 + col, "head": of},
            device_id_type=pl.DeviceIdType.MESH,
        )

    pl.when(far > 0)(lambda: greet(far - 1, near, core))
    pl.when(far < length - 1)(lambda: greet(far + 1, near, core))
    greet(far, other, core)
    if cores > 1:
        greet(far, near, 1 - core)
    lines = jnp.where(far > 0, 1, 0) + jnp.where(far < length - 1, 1, 0)
    pl.semaphore_wait(barrier, lines + (2 if cores > 1 else 1))

    mine = slot(far, near, core)
    pl.when(far < length - 1)(lambda: up(block, mine).start())
    pl.when(far > 0)(lambda: down(block, mine).start())
    across(block, mine).start()
    if cores > 1:
        beside(block, mine).start()
    keep = pltpu.make_async_copy(block, out.at[mine], own_sem)
    keep.start()

    def from_line(row, onward, more):
        at = slot(row, near, core)
        arrive(at)
        pl.when(more)(lambda: onward(out.at[at], at).start())
        across(out.at[at], at).start()
        if cores > 1:
            beside(out.at[at], at).start()

    def from_other(row):
        at = slot(row, other, core)
        arrive(at)
        if cores > 1:
            beside(out.at[at], at).start()

    for step in range(1, length + 1):
        if step < length:
            pl.when(far - step >= 0)(lambda: from_line(far - step, up, far < length - 1))
            pl.when(far + step < length)(lambda: from_line(far + step, down, far > 0))
        if step == 1:
            from_other(far)
        else:
            pl.when(far - step + 1 >= 0)(lambda: from_other(far - step + 1))
            pl.when(far + step - 1 < length)(lambda: from_other(far + step - 1))
    if cores > 1:
        for row in range(length):
            for col in range(2):
                arrive(slot(row, col, 1 - core))
    keep.wait()
    for row in range(length):
        at = slot(row, near, core)
        pl.when((row <= far) & (far < length - 1))(lambda: up(out.at[at], at).wait_send())
        pl.when((row >= far) & (far > 0))(lambda: down(out.at[at], at).wait_send())
        across(out.at[at], at).wait_send()
        if cores > 1:
            beside(out.at[at], at).wait_send()
            at = slot(row, other, core)
            beside(out.at[at], at).wait_send()


def gather(block, cores, ident):
    n_seq = lax.axis_size("seq")
    slots = n_seq * cores
    return pl.pallas_call(
        functools.partial(gather_kernel, n_seq, cores),
        out_shape=jax.ShapeDtypeStruct((slots, *block.shape), block.dtype),
        in_specs=[pl.BlockSpec(memory_space=pl.ANY)],
        out_specs=pl.BlockSpec(memory_space=pl.ANY),
        scratch_shapes=[
            pltpu.SemaphoreType.DMA,
            pltpu.SemaphoreType.DMA((4, slots)),
            pltpu.SemaphoreType.DMA((slots,)),
        ],
        compiler_params=pltpu.CompilerParams(collective_id=ident, has_side_effects=True),
    )(block)


def local(
    queries,
    keys,
    values,
    segments,
    hidden_in,
    attn_gain,
    out_proj,
    moe_gain,
    route_ids,
    route_w,
    w_gate,
    w_up,
    w_down,
):
    tok_rows = queries.shape[0]
    heads_here = attn_gain.shape[0] // DK
    query_rows = queries.reshape(tok_rows, heads_here, DK)
    key_rows = keys.reshape(tok_rows, heads_here, DK)
    value_rows = values.reshape(tok_rows, heads_here, DK)
    position = jnp.arange(tok_rows)
    causal = position[:, None] >= position[None, :]
    same_doc = (segments[:, None] == segments[None, :]) & causal
    tail_mask = (segments == segments[-1])[:, None, None]
    tail_keys = jnp.where(tail_mask, key_rows, jnp.zeros_like(key_rows))
    own_state = jnp.einsum(
        "thd,the->hde", tail_keys, value_rows, preferred_element_type=jnp.float32
    ).astype(jnp.bfloat16)
    last_seg = jnp.broadcast_to(segments[-1].astype(jnp.bfloat16), (1, DK, DK))
    payload = jnp.concatenate([own_state, last_seg], axis=0)
    gathered = gather(payload, 1, 0)
    before = jnp.arange(gathered.shape[0]) < lax.axis_index("seq")
    opened = gathered[:, heads_here, 0, 0] == segments[0].astype(jnp.bfloat16)
    keep = (before & opened)[:, None, None, None]
    prefix_state = jnp.sum(
        jnp.where(keep, gathered[:, :heads_here].astype(jnp.float32), 0.0), axis=0
    ).astype(jnp.bfloat16)
    scores = jnp.einsum("thd,shd->hts", query_rows, key_rows, preferred_element_type=jnp.float32)
    scores = jnp.where(same_doc[None], scores, 0.0).astype(jnp.bfloat16)
    local_part = jnp.einsum("hts,shd->thd", scores, value_rows, preferred_element_type=jnp.float32)
    continued = (segments == segments[0])[:, None, None]
    carried_part = jnp.einsum(
        "thd,hde->the", query_rows, prefix_state, preferred_element_type=jnp.float32
    )
    attn_raw = local_part + jnp.where(continued, carried_part, 0.0)
    mean_square = jnp.mean(attn_raw * attn_raw, axis=-1, keepdims=True)
    attended = attn_raw * lax.rsqrt(mean_square + epsilon) * attn_gain.reshape(heads_here, DK)
    attended = attended.astype(jnp.bfloat16).reshape(tok_rows, heads_here * DK)
    partial_out = jnp.dot(
        attended,
        lax.all_gather(out_proj, "seq", axis=1, tiled=True),
        preferred_element_type=jnp.float32,
    )
    attn_out = lax.psum_scatter(partial_out, "head", scatter_dimension=0, tiled=True)
    mid_wide = (hidden_in.astype(jnp.float32) + attn_out).astype(jnp.bfloat16).astype(jnp.float32)
    mid_square = jnp.mean(mid_wide * mid_wide, axis=-1, keepdims=True)
    normed = (mid_wide * lax.rsqrt(mid_square + epsilon) * moe_gain).astype(jnp.bfloat16)
    weights = route_w / jnp.sum(route_w, axis=1, keepdims=True)
    experts = lax.axis_size("seq") * lax.axis_size("head")
    labels = jnp.arange(experts, dtype=jnp.int32)
    dense = jnp.sum(
        jnp.where(route_ids[:, :, None] == labels[None, None, :], weights[:, :, None], 0.0), axis=1
    )
    everywhere = ("seq", "head")
    dense_all = lax.all_gather(dense, everywhere, axis=0, tiled=True)
    mine = lax.axis_index(everywhere)
    row_weight = jnp.sum(jnp.where(labels[None, :] == mine, dense_all, 0.0), axis=1, keepdims=True)
    rows_all = gather(normed, lax.axis_size("head"), 1).reshape(-1, normed.shape[1])
    gate_part = jnp.dot(rows_all, w_gate[0], preferred_element_type=jnp.float32)
    up_part = jnp.dot(rows_all, w_up[0], preferred_element_type=jnp.float32)
    inner = (jax.nn.silu(gate_part) * up_part).astype(jnp.bfloat16)
    answer = jnp.dot(inner, w_down[0], preferred_element_type=jnp.float32)
    answer = (answer * row_weight).astype(jnp.bfloat16)
    mixture = lax.psum_scatter(answer, everywhere, scatter_dimension=0, tiled=True)
    return (mid_wide + mixture.astype(jnp.float32)).astype(jnp.bfloat16)


def solution(mesh):
    return jax.shard_map(
        local,
        mesh=mesh,
        in_specs=(
            P(("dp", "seq"), "head"),
            P(("dp", "seq"), "head"),
            P(("dp", "seq"), "head"),
            P(("dp", "seq")),
            P(("dp", "seq", "head"), None),
            P("head"),
            P("head", "seq"),
            P(),
            P(("dp", "seq", "head"), None),
            P(("dp", "seq", "head"), None),
            P(("seq", "head"), None, None),
            P(("seq", "head"), None, None),
            P(("seq", "head"), None, None),
        ),
        out_specs=P(("dp", "seq", "head"), None),
        check_vma=False,
    )
```

```python
import functools

import jax
import jax.numpy as jnp
from jax import lax
from jax.experimental import pallas as pl
from jax.experimental.pallas import tpu as pltpu
from jax.sharding import PartitionSpec as P

D = 2048
DK = 128

epsilon = 1e-06


def gather_kernel(n_seq, cores, block, out, own_sem, send_sem, recv_sem):
    place, core = lax.axis_index("seq"), lax.axis_index("head")
    length = n_seq // 2
    far, near = place // 2, place % 2
    other = 1 - near

    def slot(row, col, of):
        return (row * 2 + col) * cores + (of if cores > 1 else 0)

    def send(way, src, at, row, col, of):
        return pltpu.make_async_remote_copy(
            src_ref=src,
            dst_ref=out.at[at],
            send_sem=send_sem.at[way, at],
            recv_sem=recv_sem.at[at],
            device_id={"seq": row * 2 + col, "head": of},
            device_id_type=pl.DeviceIdType.MESH,
        )

    def arrive(at):
        send(0, out.at[at], at, far, other, core).wait_recv()

    def up(src, at):
        return send(0, src, at, far + 1, near, core)

    def down(src, at):
        return send(1, src, at, far - 1, near, core)

    def across(src, at):
        return send(2, src, at, far, other, core)

    def beside(src, at):
        return send(3, src, at, far, near, 1 - core)

    barrier = pltpu.get_barrier_semaphore()

    def greet(row, col, of):
        pl.semaphore_signal(
            barrier,
            inc=1,
            device_id={"seq": row * 2 + col, "head": of},
            device_id_type=pl.DeviceIdType.MESH,
        )

    pl.when(far > 0)(lambda: greet(far - 1, near, core))
    pl.when(far < length - 1)(lambda: greet(far + 1, near, core))
    greet(far, other, core)
    if cores > 1:
        greet(far, near, 1 - core)
    lines = jnp.where(far > 0, 1, 0) + jnp.where(far < length - 1, 1, 0)
    pl.semaphore_wait(barrier, lines + (2 if cores > 1 else 1))

    mine = slot(far, near, core)
    pl.when(far < length - 1)(lambda: up(block, mine).start())
    pl.when(far > 0)(lambda: down(block, mine).start())
    across(block, mine).start()
    if cores > 1:
        beside(block, mine).start()
    keep = pltpu.make_async_copy(block, out.at[mine], own_sem)
    keep.start()

    def from_line(row, onward, more):
        at = slot(row, near, core)
        arrive(at)
        pl.when(more)(lambda: onward(out.at[at], at).start())
        across(out.at[at], at).start()
        if cores > 1:
            beside(out.at[at], at).start()

    def from_other(row):
        at = slot(row, other, core)
        arrive(at)
        if cores > 1:
            beside(out.at[at], at).start()

    for step in range(1, length + 1):
        if step < length:
            pl.when(far - step >= 0)(lambda: from_line(far - step, up, far < length - 1))
            pl.when(far + step < length)(lambda: from_line(far + step, down, far > 0))
        if step == 1:
            from_other(far)
        else:
            pl.when(far - step + 1 >= 0)(lambda: from_other(far - step + 1))
            pl.when(far + step - 1 < length)(lambda: from_other(far + step - 1))
    if cores > 1:
        for row in range(length):
            for col in range(2):
                arrive(slot(row, col, 1 - core))
    keep.wait()
    for row in range(length):
        at = slot(row, near, core)
        pl.when((row <= far) & (far < length - 1))(lambda: up(out.at[at], at).wait_send())
        pl.when((row >= far) & (far > 0))(lambda: down(out.at[at], at).wait_send())
        across(out.at[at], at).wait_send()
        if cores > 1:
            beside(out.at[at], at).wait_send()
            at = slot(row, other, core)
            beside(out.at[at], at).wait_send()


def gather(block, cores, ident):
    n_seq = lax.axis_size("seq")
    slots = n_seq * cores
    return pl.pallas_call(
        functools.partial(gather_kernel, n_seq, cores),
        out_shape=jax.ShapeDtypeStruct((slots, *block.shape), block.dtype),
        in_specs=[pl.BlockSpec(memory_space=pl.ANY)],
        out_specs=pl.BlockSpec(memory_space=pl.ANY),
        scratch_shapes=[
            pltpu.SemaphoreType.DMA,
            pltpu.SemaphoreType.DMA((4, slots)),
            pltpu.SemaphoreType.DMA((slots,)),
        ],
        compiler_params=pltpu.CompilerParams(collective_id=ident, has_side_effects=True),
    )(block)


def scatter_kernel(n_seq, parts, out, own, besides, across, below, above, own_sem, send_sem, recv_sem):
    place, core = lax.axis_index("seq"), lax.axis_index("head")
    length = n_seq // 2
    far, near = place // 2, place % 2
    other = 1 - near
    tall = parts.shape[1]
    piece = 16

    def far_first(visit):
        for step in range(length - 1, 0, -1):
            pl.when(far + step < length)(lambda: visit(far + step, 1))
            pl.when(far - step >= 0)(lambda: visit(far - step, -1))
        visit(far, 0)

    def send(kind, src, dst, at, row, col, of):
        return pltpu.make_async_remote_copy(
            src_ref=src,
            dst_ref=dst.at[at],
            send_sem=send_sem.at[kind, at],
            recv_sem=recv_sem.at[kind, at],
            device_id={"seq": row * 2 + col, "head": of},
            device_id_type=pl.DeviceIdType.MESH,
        )

    def to_core(row, col):
        at = row * 2 + col
        return send(0, parts.at[at * 2 + 1 - core], besides, at, far, near, 1 - core)

    def to_near(row):
        return send(1, besides.at[row * 2 + other], across, row, far, other, core)

    def go_up(row):
        return send(2, besides.at[row * 2 + near], below, row, far + 1, near, core)

    def go_down(row):
        return send(3, besides.at[row * 2 + near], above, row, far - 1, near, core)

    def load(row, col):
        at = row * 2 + col
        return pltpu.make_async_copy(parts.at[at * 2 + core], own.at[at], own_sem.at[at])

    def add(target, *terms):
        @pl.loop(0, tall // piece)
        def _(turn):
            rows = pl.ds(pl.multiple_of(turn * piece, piece), piece)
            total = target[rows, :].astype(jnp.float32)
            for term in terms:
                total = total + term[rows, :].astype(jnp.float32)
            target[rows, :] = total.astype(target.dtype)

    barrier = pltpu.get_barrier_semaphore()

    def greet(row, col, of):
        pl.semaphore_signal(
            barrier,
            inc=1,
            device_id={"seq": row * 2 + col, "head": of},
            device_id_type=pl.DeviceIdType.MESH,
        )

    pl.when(far > 0)(lambda: greet(far - 1, near, core))
    pl.when(far < length - 1)(lambda: greet(far + 1, near, core))
    greet(far, other, core)
    greet(far, near, 1 - core)
    lines = jnp.where(far > 0, 1, 0) + jnp.where(far < length - 1, 1, 0)
    pl.semaphore_wait(barrier, lines + 2)

    def begin(col):
        def visit(row, side):
            to_core(row, col).start()
            load(row, col).start()

        return visit

    far_first(begin(other))
    far_first(begin(near))

    def first(row, side):
        at = row * 2 + other
        load(row, other).wait()
        to_core(row, other).wait_recv()
        add(besides.at[at], own.at[at])
        to_near(row).start()

    def second(row, side):
        at = row * 2 + near
        load(row, near).wait()
        to_core(row, near).wait_recv()
        to_near(row).wait_recv()
        add(besides.at[at], own.at[at], across.at[row])
        if side >= 0:

            @pl.when(far > 0)
            def _():
                go_up(row).wait_recv()
                add(besides.at[at], below.at[row])

            if side > 0:
                go_up(row).start()
        if side <= 0:

            @pl.when(far < length - 1)
            def _():
                go_down(row).wait_recv()
                add(besides.at[at], above.at[row])

            if side < 0:
                go_down(row).start()

    far_first(first)
    far_first(second)
    out[...] = besides[far * 2 + near]

    def finish(row, side):
        to_core(row, other).wait_send()
        to_core(row, near).wait_send()
        to_near(row).wait_send()
        if side > 0:
            go_up(row).wait_send()
        if side < 0:
            go_down(row).wait_send()

    far_first(finish)


def scatter_sum(parts, ident):
    n_seq = lax.axis_size("seq")
    slots, tall, wide = parts.shape
    length = n_seq // 2
    held = [(n_seq, tall, wide)] * 2 + [(length, tall, wide)] * 3
    taken = sum(n for n, _, _ in held) * tall * wide * parts.dtype.itemsize
    return pl.pallas_call(
        functools.partial(scatter_kernel, n_seq),
        out_shape=jax.ShapeDtypeStruct((tall, wide), parts.dtype),
        in_specs=[pl.BlockSpec(memory_space=pl.ANY)],
        out_specs=pl.BlockSpec(memory_space=pltpu.VMEM),
        scratch_shapes=[pltpu.VMEM(shape, parts.dtype) for shape in held]
        + [
            pltpu.SemaphoreType.DMA((n_seq,)),
            pltpu.SemaphoreType.DMA((4, n_seq)),
            pltpu.SemaphoreType.DMA((4, n_seq)),
        ],
        compiler_params=pltpu.CompilerParams(
            collective_id=ident, has_side_effects=True, vmem_limit_bytes=taken + (4 << 20)
        ),
    )(parts)


def local(
    queries,
    keys,
    values,
    segments,
    hidden_in,
    attn_gain,
    out_proj,
    moe_gain,
    route_ids,
    route_w,
    w_gate,
    w_up,
    w_down,
):
    tok_rows = queries.shape[0]
    heads_here = attn_gain.shape[0] // DK
    query_rows = queries.reshape(tok_rows, heads_here, DK)
    key_rows = keys.reshape(tok_rows, heads_here, DK)
    value_rows = values.reshape(tok_rows, heads_here, DK)
    position = jnp.arange(tok_rows)
    causal = position[:, None] >= position[None, :]
    same_doc = (segments[:, None] == segments[None, :]) & causal
    tail_mask = (segments == segments[-1])[:, None, None]
    tail_keys = jnp.where(tail_mask, key_rows, jnp.zeros_like(key_rows))
    own_state = jnp.einsum(
        "thd,the->hde", tail_keys, value_rows, preferred_element_type=jnp.float32
    ).astype(jnp.bfloat16)
    last_seg = jnp.broadcast_to(segments[-1].astype(jnp.bfloat16), (1, DK, DK))
    payload = jnp.concatenate([own_state, last_seg], axis=0)
    gathered = gather(payload, 1, 0)
    before = jnp.arange(gathered.shape[0]) < lax.axis_index("seq")
    opened = gathered[:, heads_here, 0, 0] == segments[0].astype(jnp.bfloat16)
    keep = (before & opened)[:, None, None, None]
    prefix_state = jnp.sum(
        jnp.where(keep, gathered[:, :heads_here].astype(jnp.float32), 0.0), axis=0
    ).astype(jnp.bfloat16)
    scores = jnp.einsum("thd,shd->hts", query_rows, key_rows, preferred_element_type=jnp.float32)
    scores = jnp.where(same_doc[None], scores, 0.0).astype(jnp.bfloat16)
    local_part = jnp.einsum("hts,shd->thd", scores, value_rows, preferred_element_type=jnp.float32)
    continued = (segments == segments[0])[:, None, None]
    carried_part = jnp.einsum(
        "thd,hde->the", query_rows, prefix_state, preferred_element_type=jnp.float32
    )
    attn_raw = local_part + jnp.where(continued, carried_part, 0.0)
    mean_square = jnp.mean(attn_raw * attn_raw, axis=-1, keepdims=True)
    attended = attn_raw * lax.rsqrt(mean_square + epsilon) * attn_gain.reshape(heads_here, DK)
    attended = attended.astype(jnp.bfloat16).reshape(tok_rows, heads_here * DK)
    partial_out = jnp.dot(
        attended,
        lax.all_gather(out_proj, "seq", axis=1, tiled=True),
        preferred_element_type=jnp.float32,
    )
    attn_out = lax.psum_scatter(partial_out, "head", scatter_dimension=0, tiled=True)
    mid_wide = (hidden_in.astype(jnp.float32) + attn_out).astype(jnp.bfloat16).astype(jnp.float32)
    mid_square = jnp.mean(mid_wide * mid_wide, axis=-1, keepdims=True)
    normed = (mid_wide * lax.rsqrt(mid_square + epsilon) * moe_gain).astype(jnp.bfloat16)
    weights = route_w / jnp.sum(route_w, axis=1, keepdims=True)
    experts = lax.axis_size("seq") * lax.axis_size("head")
    labels = jnp.arange(experts, dtype=jnp.int32)
    dense = jnp.sum(
        jnp.where(route_ids[:, :, None] == labels[None, None, :], weights[:, :, None], 0.0), axis=1
    )
    everywhere = ("seq", "head")
    dense_all = lax.all_gather(dense, everywhere, axis=0, tiled=True)
    mine = lax.axis_index(everywhere)
    row_weight = jnp.sum(jnp.where(labels[None, :] == mine, dense_all, 0.0), axis=1, keepdims=True)
    rows_all = gather(normed, lax.axis_size("head"), 1).reshape(-1, normed.shape[1])
    gate_part = jnp.dot(rows_all, w_gate[0], preferred_element_type=jnp.float32)
    up_part = jnp.dot(rows_all, w_up[0], preferred_element_type=jnp.float32)
    inner = (jax.nn.silu(gate_part) * up_part).astype(jnp.bfloat16)
    answer = jnp.dot(inner, w_down[0], preferred_element_type=jnp.float32)
    answer = (answer * row_weight).astype(jnp.bfloat16)
    mixture = scatter_sum(answer.reshape(experts, -1, D), 2)
    return (mid_wide + mixture.astype(jnp.float32)).astype(jnp.bfloat16)


def solution(mesh):
    return jax.shard_map(
        local,
        mesh=mesh,
        in_specs=(
            P(("dp", "seq"), "head"),
            P(("dp", "seq"), "head"),
            P(("dp", "seq"), "head"),
            P(("dp", "seq")),
            P(("dp", "seq", "head"), None),
            P("head"),
            P("head", "seq"),
            P(),
            P(("dp", "seq", "head"), None),
            P(("dp", "seq", "head"), None),
            P(("seq", "head"), None, None),
            P(("seq", "head"), None, None),
            P(("seq", "head"), None, None),
        ),
        out_specs=P(("dp", "seq", "head"), None),
        check_vma=False,
    )
```
